512 devices in a mesh: obs: 16 (over y, core), chan: 32 (over x, z).
Axes of the slice: x: 4, y: 8, z: 8, core: 2. Of those that a mesh axis runs over, the one named last changes fastest.
Arguments:
- visibilities: bfloat16 [16, 64, 384, 2, 2, 256], P('obs', None, 'chan'), may hold values from -6 to 6
- weights: int32 [16, 64, 384, 2], P('obs', None, 'chan'), may hold values from 0 to 16
- coverage: int32 [16, 64], P('obs'), may hold values from 0 to 255, as said below
- owner_map: int32 [256], replicated, may hold values from 0 to 255, as said below
Outputs:
- delay_cube: float32 [256, 2, 2, 256, 384], P('obs', None, None, 'chan')
The draws below stay inside these ranges and needn't reach their ends.
Inputs may be any that keep to these rules, and one draw needn't show every extreme that they name: `coverage`: each row lists 64 different tiles. Of one observation's tiles at most 6 are held by one owner, the owner o holding the tiles owner_map[o * 16] to owner_map[(o + 1) * 16 - 1]; in every observation some owner holds exactly 6 of them. `owner_map`: A permutation of the tile numbers.
All inputs are finite; a program needn't handle non-finite values.
Results may differ from the reference program's by a relative error of at most 0.0037.
Values may be sent and summed in bfloat16 or wider, within the bound.
A program may use at most 128 MiB of HBM per device.

```python
import math
import jax
import jax.numpy as jnp
from jax import lax

NCHAN = 384
CELLS = 256
NT = 256
POL = 2
OCC = 64
NOBS = 16
TPO = 16
CAP = 6


def season_layout(key):
    owner_map = jax.random.permutation(jax.random.fold_in(key, 11), NT).astype(jnp.int32)
    owners = NT // TPO
    popular = jax.random.randint(jax.random.fold_in(key, 12), (owners,), 0, 4)
    forced = jax.random.randint(jax.random.fold_in(key, 13), (NOBS,), 0, owners)
    noise_seed_key = jax.random.split(jax.random.fold_in(key, 14), NOBS)
    noise = jax.vmap(lambda sub: jax.random.permutation(sub, owners * CAP))(noise_seed_key).astype(jnp.int32)
    owner_ids = jnp.arange(owners, dtype=jnp.int32)
    priority = popular[None, :] + 8 * (owner_ids[None, :] == forced[:, None]).astype(jnp.int32)
    priority = jnp.broadcast_to(priority[:, :, None], (NOBS, owners, CAP)).reshape(NOBS, owners * CAP)
    ranking_scores = priority * (owners * CAP) + noise
    pick_keys = jax.random.split(jax.random.fold_in(key, 15), NOBS * owners)
    within = jax.vmap(lambda sub: jax.random.permutation(sub, TPO))(pick_keys).astype(jnp.int32)
    within = within.reshape(NOBS, owners, TPO)[:, :, :CAP]
    candidates = owner_map[owner_ids[None, :, None] * TPO + within].reshape(NOBS, owners * CAP)
    chosen = jax.lax.top_k(ranking_scores, OCC)[1]
    listed = jnp.take_along_axis(candidates, chosen, axis=1)
    order_keys = jax.random.split(jax.random.fold_in(key, 16), NOBS)
    shuffle = jax.vmap(lambda sub: jax.random.permutation(sub, OCC))(order_keys)
    coverage = jnp.take_along_axis(listed, shuffle, axis=1).astype(jnp.int32)
    return (owner_map, coverage)


def draw_coverage(key, part):
    return season_layout(key)[1]


def draw_owner_map(key, part):
    return season_layout(key)[0]


def plant(values, own_key, low, largest):
    index_at = [jax.random.randint(jax.random.fold_in(own_key, axis), (), 0, length) for axis, length in enumerate(values.shape)]
    widest = values.shape.index(max(values.shape))
    next_to = index_at[:widest] + [(index_at[widest] + 1) % values.shape[widest]] + index_at[widest + 1:]
    return values.at[tuple(index_at)].set(low).at[tuple(next_to)].set(largest)


def steps_of(stream_key, shape, cuts, smallest, largest):
    loudness = 1.0
    for axis_at, blocks in cuts:
        steps = jax.random.uniform(jax.random.fold_in(jax.random.fold_in(stream_key, 6), axis_at), (blocks,), jnp.float32, smallest / len(cuts), largest / len(cuts))
        loudness = loudness * jnp.repeat(jnp.exp(steps), shape[axis_at] // blocks).reshape((-1,) + (1,) * (len(shape) - 1 - axis_at))
    return loudness


def gaussian(own_key, shape, scale, most, cuts=(), kind=jnp.bfloat16):
    result = scale * jax.random.normal(own_key, shape, jnp.float32)
    if cuts:
        result = result * steps_of(own_key, shape, cuts, -0.22, 0.18)
    return jnp.clip(result, -most, most).astype(kind)


def setup_inputs(seed: int = 0) -> dict:
    key_list = jax.random.split(jax.random.key(seed), 5)
    return {
        "visibilities": gaussian(key_list[0], (NOBS, OCC, NCHAN, POL, 2, CELLS), 1.0, 6.0, ((0, 16), (2, 32))),
        "weights": plant(jax.random.randint(key_list[1], (NOBS, OCC, NCHAN, POL), 0, 17), jax.random.fold_in(key_list[1], 1), 0, 16).astype(jnp.int32),
        "coverage": draw_coverage(jax.random.fold_in(key_list[4], 71), 0),
        "owner_map": draw_owner_map(jax.random.fold_in(key_list[4], 71), 0),
    }


harris_terms = (0.35875, 0.48829, 0.14128, 0.01168)

def delay_table(length):
    index = jnp.arange(length, dtype=jnp.int32)
    phase = index[:, None] * index[None, :] % length
    angle = 2.0 * math.pi / length * phase.astype(jnp.float32)
    base = 2.0 * math.pi / (length - 1) * index.astype(jnp.float32)
    taper = harris_terms[0] - harris_terms[1] * jnp.cos(base) + harris_terms[2] * jnp.cos(2.0 * base) - harris_terms[3] * jnp.cos(3.0 * base)
    column = (taper / math.sqrt(length))[:, None]
    cosine = column * jnp.cos(angle)
    sine = column * jnp.sin(angle)
    table = jnp.stack([jnp.stack([cosine, -sine], 1), jnp.stack([sine, cosine], 1)], 0)
    return table.astype(jnp.bfloat16)

def reference(visibilities, weights, coverage, owner_map):
    tiles_total = owner_map.shape[0]
    matches = coverage[:, :, None] == owner_map[None, None, :]
    places = lax.optimization_barrier(jnp.sum(jnp.where(matches, jnp.arange(tiles_total, dtype=jnp.int32), 0), axis=-1)).astype(jnp.int32)
    shape_grid = (tiles_total,) + visibilities.shape[2:]
    shape_total = (tiles_total,) + weights.shape[2:]

    def add_one(carry, pieces):
        place, vis, wts = pieces
        weight_float = wts.astype(jnp.float32)
        scaled_values = weight_float[..., None, None] * vis.astype(jnp.float32)
        return ((carry[0].at[place].add(scaled_values), carry[1].at[place].add(weight_float)), None)
    start = (jnp.zeros(shape_grid, jnp.float32), jnp.zeros(shape_total, jnp.float32))
    (grid, total), _ = lax.scan(add_one, start, (places, visibilities, weights))
    normalized = (grid / jnp.maximum(total, 1.0)[..., None, None]).astype(jnp.bfloat16)
    table = delay_table(NCHAN)
    return jnp.einsum('tnpal,anbq->tpblq', normalized.astype(jnp.float32), table.astype(jnp.float32), precision=lax.Precision.HIGHEST)
```

```python
import functools
import math

import jax
import jax.numpy as jnp
import ml_dtypes
import numpy as np
from jax import lax
from jax.experimental import pallas as pl
from jax.experimental.pallas import tpu as pltpu
from jax.sharding import PartitionSpec as P

F32, BF16, I32 = jnp.float32, jnp.bfloat16, jnp.int32
MESH = pl.DeviceIdType.MESH

NCHAN = 384
OCC = 64
TPO = 16
HALF = 8
NX, NY, NZ = 4, 8, 8
NCH = NX * NZ
LOCAL = NCHAN // NCH
PARTS = 3
CPP = LOCAL // PARTS
ROWS = CPP * 8
RIGHT, LEFT = 0, 1


def hops(way, half):
    return 4 if way == half else 3


def delay_table():
    n = np.arange(NCHAN)
    angle = 2.0 * math.pi * (np.outer(n, n) % NCHAN) / NCHAN
    base = 2.0 * math.pi * n / (NCHAN - 1)
    taper = 0.35875 - 0.48829 * np.cos(base) + 0.14128 * np.cos(2 * base) - 0.01168 * np.cos(3 * base)
    column = (taper / math.sqrt(NCHAN))[:, None]
    cosine, sine = column * np.cos(angle), column * np.sin(angle)
    table = np.stack([np.stack([cosine, -sine], 1), np.stack([sine, cosine], 1)], 0)
    table = table.astype(np.float32).astype(ml_dtypes.bfloat16)
    table = table.reshape(2, NCH, PARTS, CPP, 2 * NCHAN).transpose(2, 1, 3, 0, 4)
    return table.reshape(PARTS, NCH * CPP * 2, 2 * NCHAN)


def swap(lo, hi, mask, shift, axis):
    size = lo.shape[axis]
    new_lo = jnp.where(mask, pltpu.roll(hi, shift, axis), lo)
    new_hi = jnp.where(mask, hi, pltpu.roll(lo, size - shift, axis))
    return new_lo, new_hi


def block_transpose(blocks, unit, axis):
    blocks = list(blocks)
    group = lax.broadcasted_iota(I32, blocks[0].shape, axis) // unit
    step = 1
    while step < len(blocks):
        mask = (group // step) % 2 == 1
        for i in range(len(blocks)):
            if (i // step) % 2 == 0:
                blocks[i], blocks[i + step] = swap(blocks[i], blocks[i + step], mask, unit * step, axis)
        step *= 2
    return blocks


def kernel(
    vis, rw, inv, inv_v, tab, out,
    v0, v1, rw1, inv1_v, inv1, scaled, wt, tsend, trecv, tloc, rinv, send, recv, norm, mixed, outbox, inbox, tabv,
    s_v0, s_tab, s_inv, s_sib_s, s_sib_r, s_small_s, s_small_r, s_tot_s, s_tot_r, s_ring_s, s_ring_r, s_a2a_s, s_a2a_r,
):
    ob = lax.axis_index("obs")
    ch = lax.axis_index("chan")
    y, core = ob // 2, ob % 2
    x, z = ch // NZ, ch % NZ
    sibling = (y * 2 + 1 - core, ch)
    beside = {RIGHT: (((y + 1) % NY) * 2 + core, ch), LEFT: (((y + NY - 1) % NY) * 2 + core, ch)}

    def peer(d):
        return ((x + d // NZ) % NX) * NZ + (z + d % NZ) % NZ

    barrier = pltpu.get_barrier_semaphore()
    for device in (sibling, beside[RIGHT], beside[LEFT]):
        pl.semaphore_signal(barrier, inc=1, device_id=device, device_id_type=MESH)

    def greet(d, carry):
        pl.semaphore_signal(barrier, inc=1, device_id=(ob, peer(d)), device_id_type=MESH)
        return carry

    lax.fori_loop(1, NCH, greet, 0)

    load = [pltpu.make_async_copy(vis.at[:, pl.ds(s * ROWS, ROWS), :], v0.at[s], s_v0.at[s]) for s in range(PARTS)]
    load_tab = pltpu.make_async_copy(tab, tabv, s_tab)
    for copy in load:
        copy.start()
    load_tab.start()
    pl.semaphore_wait(barrier, NCH + 2)

    def remote(src, dst, s_sem, r_sem, device):
        return pltpu.make_async_remote_copy(
            src_ref=src, dst_ref=dst, send_sem=s_sem, recv_sem=r_sem, device_id=device, device_id_type=MESH
        )

    swaps = [
        remote(vis.at[:, pl.ds(s * ROWS, ROWS), :], v1.at[s], s_sib_s.at[s], s_sib_r.at[s], sibling) for s in range(PARTS)
    ]
    swap_rw = remote(rw, rw1, s_small_s.at[0], s_small_r.at[0], sibling)
    swap_inv = remote(inv_v, inv1_v, s_small_s.at[1], s_small_r.at[1], sibling)
    swap_inv.start()
    swap_rw.start()
    for copy in swaps:
        copy.start()

    for s in range(PARTS):
        for o in range(2):
            scaled[s, o, OCC] = jnp.zeros((ROWS, 128), F32)
    rinv[...] = jnp.zeros((128, 128), F32)
    wt[0] = rw[...].T
    swap_inv.wait_recv()
    to_smem = pltpu.make_async_copy(inv1_v, inv1, s_inv)
    to_smem.start()
    swap_rw.wait_recv()
    wt[1] = rw1[...].T
    to_smem.wait()

    def scale(s):
        for o, (v, w) in enumerate(((v0, rw), (v1, rw1))):
            if o == 0:
                load[s].wait()
            else:
                swaps[s].wait_recv()

            def body(g, weights):
                for j in range(4):
                    column = jnp.broadcast_to(weights[:, j : j + 1], (ROWS, 128))
                    scaled[s, o, g * 4 + j] = v[s, g * 4 + j].astype(F32) * column
                return pltpu.roll(weights, 124, 1)

            lax.fori_loop(0, OCC // 4, body, w[pl.ds(s * ROWS, ROWS), :])

    def slots(owner_y, i):
        t = (owner_y * 2 + core) * TPO + i
        return inv[t // 128, t % 128], inv1[t // 128, t % 128]

    def local(s, owner_y, i):
        k0, k1 = slots(owner_y, i)
        return scaled[s, 0, k0] + scaled[s, 1, k1]

    def owner_of(way, h, n):
        away = n - h + 1
        return (y + away) % NY if way == RIGHT else (y + NY - away) % NY

    ring, totals = {}, {}

    def emit(s, way, half, h):
        n = hops(way, half)
        owner = owner_of(way, h, n)
        if h > 1:
            ring[s, way, half, h - 1].wait_recv()

        def body(g, carry):
            for j in range(4):
                i = g * 4 + j
                acc = local(s, owner, half * HALF + i)
                if h > 1:
                    acc = acc + recv[s, way, half, h - 2, i].astype(F32)
                send[s, way, half, h - 1, i] = acc.astype(BF16)
            return carry

        lax.fori_loop(0, HALF // 4, body, 0)
        copy = remote(
            send.at[s, way, half, h - 1], recv.at[s, way, half, h - 1],
            s_ring_s.at[s, way, half, h - 1], s_ring_r.at[s, way, half, h - 1], beside[way],
        )
        copy.start()
        ring[s, way, half, h] = copy

    def local_totals(owner):
        def body(i, carry):
            k0, k1 = slots(owner, i)
            tloc[pl.ds(i, 1), :] = wt[0, pl.ds(k0, 1), :] + wt[1, pl.ds(k1, 1), :]
            return carry

        lax.fori_loop(0, TPO, body, 0)
        return tloc[...]

    def emit_total(way, h):
        n = hops(way, 0)
        acc = local_totals(owner_of(way, h, n))
        if h > 1:
            totals[way, h - 1].wait_recv()
            acc = acc + trecv[way, h - 2].astype(F32)
        tsend[way, h - 1] = acc.astype(BF16)
        copy = remote(
            tsend.at[way, h - 1], trecv.at[way, h - 1], s_tot_s.at[way, h - 1], s_tot_r.at[way, h - 1], beside[way]
        )
        copy.start()
        totals[way, h] = copy

    def total_inverse():
        acc = local_totals(y)
        for way in (RIGHT, LEFT):
            n = hops(way, 0)
            totals[way, n].wait_recv()
            acc = acc + trecv[way, n - 1].astype(F32)
        rinv[0:TPO, :] = 1.0 / jnp.maximum(acc, 1.0)
        rinv[...] = rinv[...].T

    sends = []

    def finish(s):
        factor = rinv[pl.ds(s * ROWS, ROWS), :]
        for half in range(2):
            for way in (RIGHT, LEFT):
                ring[s, way, half, hops(way, half)].wait_recv()
            for j in range(HALF):
                i = half * HALF + j
                acc = local(s, y, i)
                for way in (RIGHT, LEFT):
                    acc = acc + recv[s, way, half, hops(way, half) - 1, j].astype(F32)
                norm[i] = acc * jnp.broadcast_to(factor[:, i : i + 1], (ROWS, 128))

        def lanes(c, carry):
            blocks = [norm[i, pl.ds(c * 8, 8), :] for i in range(TPO)]
            for g, block in enumerate(block_transpose(blocks, 8, 1)):
                mixed[g, c] = block
            return carry

        lax.fori_loop(0, CPP, lanes, 0)

        def sublanes(g, carry):
            parts = block_transpose([mixed[g, c] for c in range(CPP)], 2, 0)
            for lh in range(2):
                outbox[s, lh * 16 + g] = jnp.concatenate([parts[lh], parts[2 + lh]], 0).astype(BF16)
            return carry

        lax.fori_loop(0, 16, sublanes, 0)

        def post(d, carry):
            to = peer(d)
            remote(outbox.at[s, to], inbox.at[s, ch], s_a2a_s.at[s], s_a2a_r.at[s], (ob, to)).start()
            return carry

        lax.fori_loop(1, NCH, post, 0)
        inbox[s, ch] = outbox[s, ch]

    def all_of(box, s, sem):
        some = box.at[s, pl.ds(0, NCH - 1)]
        return pltpu.make_async_copy(some, some, sem)

    def transform(s):
        all_of(inbox, s, s_a2a_r.at[s]).wait()
        if s == 0:
            load_tab.wait()
        cells = inbox[s].astype(F32).reshape(NCH, 2, 8, 128)
        for p in range(2):
            left = cells[:, p].reshape(NCH * 8, 128).T.astype(BF16)
            product = jnp.dot(left, tabv[s], preferred_element_type=F32)
            for b in range(2):
                block = product[:, b * NCHAN : (b + 1) * NCHAN].reshape(TPO, 8, NCHAN)
                out[:, p, b] = block if s == 0 else out[:, p, b] + block

    for tick in range(PARTS + 4):
        if tick < PARTS:
            scale(tick)
        for h in range(1, 5):
            s = tick - h + 1
            if 0 <= s < PARTS:
                for half in range(2):
                    for way in (RIGHT, LEFT):
                        if h <= hops(way, half):
                            emit(s, way, half, h)
                if s == 0:
                    for way in (RIGHT, LEFT):
                        if h <= hops(way, 0):
                            emit_total(way, h)
        if tick == 4:
            total_inverse()
        if tick >= 4:
            finish(tick - 4)
        if tick >= 5:
            transform(tick - 5)
    transform(PARTS - 1)

    for copy in [*swaps, swap_rw, swap_inv, *ring.values(), *totals.values()]:
        copy.wait_send()
    for s in range(PARTS):
        all_of(outbox, s, s_a2a_s.at[s]).wait()


def shards(visibilities, weights, coverage, owner_map):
    vis = visibilities.reshape(OCC, LOCAL, 2, 2, 2, 128).transpose(0, 1, 2, 4, 3, 5).reshape(OCC, LOCAL * 8, 128)
    rw = jnp.repeat(weights[0].transpose(1, 2, 0).reshape(LOCAL * 2, OCC), 4, axis=0).astype(F32)
    rw = jnp.pad(rw, ((0, 128 - LOCAL * 8), (0, 128 - OCC)))
    same = owner_map[:, None] == coverage[0][None, :]
    inv = OCC + jnp.sum(jnp.where(same, jnp.arange(OCC, dtype=I32) - OCC, 0), axis=1).astype(I32)
    inv = inv.reshape(2, 128)
    table = jnp.asarray(delay_table())

    vmem, smem, anywhere = (pl.BlockSpec(memory_space=m) for m in (pltpu.VMEM, pltpu.SMEM, pl.ANY))
    dma = pltpu.SemaphoreType.DMA
    return pl.pallas_call(
        kernel,
        out_shape=jax.ShapeDtypeStruct((TPO, 2, 2, 8, NCHAN), F32),
        in_specs=[anywhere, vmem, smem, vmem, anywhere],
        out_specs=vmem,
        scratch_shapes=[
            pltpu.VMEM((PARTS, OCC, ROWS, 128), BF16),
            pltpu.VMEM((PARTS, OCC, ROWS, 128), BF16),
            pltpu.VMEM((128, 128), F32),
            pltpu.VMEM((2, 128), I32),
            pltpu.SMEM((2, 128), I32),
            pltpu.VMEM((PARTS, 2, OCC + 1, ROWS, 128), F32),
            pltpu.VMEM((2, 128, 128), F32),
            pltpu.VMEM((2, 4, TPO, 128), BF16),
            pltpu.VMEM((2, 4, TPO, 128), BF16),
            pltpu.VMEM((TPO, 128), F32),
            pltpu.VMEM((128, 128), F32),
            pltpu.VMEM((PARTS, 2, 2, 4, HALF, ROWS, 128), BF16),
            pltpu.VMEM((PARTS, 2, 2, 4, HALF, ROWS, 128), BF16),
            pltpu.VMEM((TPO, ROWS, 128), F32),
            pltpu.VMEM((16, CPP, 8, 128), F32),
            pltpu.VMEM((PARTS, NCH, 16, 128), BF16),
            pltpu.VMEM((PARTS, NCH, 16, 128), BF16),
            pltpu.VMEM(table.shape, BF16),
            dma((PARTS,)),
            dma,
            dma,
            dma((PARTS,)),
            dma((PARTS,)),
            dma((2,)),
            dma((2,)),
            dma((2, 4)),
            dma((2, 4)),
            dma((PARTS, 2, 2, 4)),
            dma((PARTS, 2, 2, 4)),
            dma((PARTS,)),
            dma((PARTS,)),
        ],
        compiler_params=pltpu.CompilerParams(
            collective_id=0, has_side_effects=True, vmem_limit_bytes=48 * 1024 * 1024
        ),
    )(vis, rw, inv, inv, table)


def solution(mesh):
    return jax.shard_map(
        shards,
        mesh=mesh,
        in_specs=(
            P("obs", None, "chan", None, None, None),
            P("obs", None, "chan", None),
            P("obs", None),
            P(),
        ),
        out_specs=P("obs", None, None, "chan", None),
        check_vma=False,
    )
```

```python
import functools
import math

import jax
import jax.numpy as jnp
import ml_dtypes
import numpy as np
from jax import lax
from jax.experimental import pallas as pl
from jax.experimental.pallas import tpu as pltpu
from jax.sharding import PartitionSpec as P

F32, BF16, I32 = jnp.float32, jnp.bfloat16, jnp.int32
MESH = pl.DeviceIdType.MESH

NCHAN = 384
OCC = 64
TPO = 16
HALF = 8
NX, NY, NZ = 4, 8, 8
NCH = NX * NZ
LOCAL = NCHAN // NCH
PARTS = 3
CPP = LOCAL // PARTS
ROWS = CPP * 8
RIGHT, LEFT = 0, 1


def hops(way, half):
    return 4 if way == half else 3


def delay_table():
    n = np.arange(NCHAN)
    angle = 2.0 * math.pi * (np.outer(n, n) % NCHAN) / NCHAN
    base = 2.0 * math.pi * n / (NCHAN - 1)
    taper = 0.35875 - 0.48829 * np.cos(base) + 0.14128 * np.cos(2 * base) - 0.01168 * np.cos(3 * base)
    column = (taper / math.sqrt(NCHAN))[:, None]
    cosine, sine = column * np.cos(angle), column * np.sin(angle)
    table = np.stack([np.stack([cosine, -sine], 1), np.stack([sine, cosine], 1)], 0)
    table = table.astype(np.float32).astype(ml_dtypes.bfloat16)
    table = table.reshape(2, NCH, PARTS, CPP, 2 * NCHAN).transpose(2, 1, 3, 0, 4)
    table = table.reshape(PARTS, NCH * CPP * 2, 2 * NCHAN // 128, 128)
    return table.transpose(0, 2, 1, 3)


def swap(lo, hi, mask, shift, axis):
    size = lo.shape[axis]
    new_lo = jnp.where(mask, pltpu.roll(hi, shift, axis), lo)
    new_hi = jnp.where(mask, hi, pltpu.roll(lo, size - shift, axis))
    return new_lo, new_hi


def block_transpose(blocks, unit, axis):
    blocks = list(blocks)
    group = lax.broadcasted_iota(I32, blocks[0].shape, axis) // unit
    step = 1
    while step < len(blocks):
        mask = (group // step) % 2 == 1
        for i in range(len(blocks)):
            if (i // step) % 2 == 0:
                blocks[i], blocks[i + step] = swap(blocks[i], blocks[i + step], mask, unit * step, axis)
        step *= 2
    return blocks


def kernel(
    vis, weights, coverage, owner_map, tab, out,
    v0, v1, rw, rolled, slot_v, slot, tile_totals, scaled, tsend, trecv, rinv, send, recv, norm, mixed, outbox, inbox, tabv,
    s_v0, s_tab, s_inv, s_sib_s, s_sib_r, s_small_s, s_small_r, s_tot_s, s_tot_r, s_ring_s, s_ring_r, s_a2a_s, s_a2a_r,
):
    ob = lax.axis_index("obs")
    ch = lax.axis_index("chan")
    y, core = ob // 2, ob % 2
    x, z = ch // NZ, ch % NZ
    sibling = (y * 2 + 1 - core, ch)
    beside = {RIGHT: (((y + 1) % NY) * 2 + core, ch), LEFT: (((y + NY - 1) % NY) * 2 + core, ch)}

    def peer(d):
        return ((x + d // NZ) % NX) * NZ + (z + d % NZ) % NZ

    barrier = pltpu.get_barrier_semaphore()
    for device in (sibling, beside[RIGHT], beside[LEFT]):
        pl.semaphore_signal(barrier, inc=1, device_id=device, device_id_type=MESH)

    def greet(d, carry):
        pl.semaphore_signal(barrier, inc=1, device_id=(ob, peer(d)), device_id_type=MESH)
        return carry

    lax.fori_loop(1, NCH, greet, 0)

    load = [pltpu.make_async_copy(vis.at[:, pl.ds(s * ROWS, ROWS), :], v0.at[s], s_v0.at[s]) for s in range(PARTS)]
    load_tab = pltpu.make_async_copy(tab, tabv, s_tab)
    for copy in load:
        copy.start()
    load_tab.start()

    rw[0] = jnp.zeros((128, 128), F32)
    first = lax.broadcasted_iota(I32, (8, OCC), 0) < 4
    for c in range(LOCAL):
        pair = weights[c].astype(F32)
        rw[0, c * 8 : (c + 1) * 8, 0:OCC] = jnp.where(first, pair[0:1], pair[1:2])
    rinv[...] = jnp.zeros((128, 128), F32)
    rinv[:, 0:OCC] = jnp.broadcast_to(coverage[...].astype(F32), (128, OCC))
    listed = rinv[...].T
    k = lax.broadcasted_iota(I32, (128, 128), 0)
    for part in range(2):
        same = (listed == owner_map[part : part + 1, :].astype(F32)) & (k < OCC)
        slot_v[0, part : part + 1, :] = jnp.min(jnp.where(same, k, OCC), axis=0, keepdims=True)
        totals_t = jnp.dot(rw[0].astype(BF16), same.astype(F32).astype(BF16), preferred_element_type=F32)
        tile_totals[0, pl.ds(part * 128, 128), :] = totals_t.T

    def roll_weights(o):
        for g in range(4):
            rolled[o, g] = rw[o] if g == 0 else pltpu.roll(rw[o], 128 - 16 * g, 1)

    roll_weights(0)
    for s in range(PARTS):
        for o in range(2):
            scaled[s, o, OCC] = jnp.zeros((ROWS, 128), F32)
    pl.semaphore_wait(barrier, NCH + 2)

    def remote(src, dst, s_sem, r_sem, device):
        return pltpu.make_async_remote_copy(
            src_ref=src, dst_ref=dst, send_sem=s_sem, recv_sem=r_sem, device_id=device, device_id_type=MESH
        )

    swaps = [
        remote(vis.at[:, pl.ds(s * ROWS, ROWS), :], v1.at[s], s_sib_s.at[s], s_sib_r.at[s], sibling) for s in range(PARTS)
    ]
    smalls = [
        remote(box.at[0], box.at[1], s_small_s.at[i], s_small_r.at[i], sibling)
        for i, box in enumerate((slot_v, rw, tile_totals))
    ]
    smalls[0].start()
    smalls[1].start()
    swaps[0].start()
    smalls[2].start()
    for copy in swaps[1:]:
        copy.start()
    to_smem = [pltpu.make_async_copy(slot_v.at[o], slot.at[o], s_inv.at[o]) for o in range(2)]
    to_smem[0].start()

    def scale(s, o):
        v = (v0, v1)[o]

        def body(g, carry):
            columns = rolled[o, g, pl.ds(s * ROWS, ROWS), :]
            for j in range(16):
                column = jnp.broadcast_to(columns[:, j : j + 1], (ROWS, 128))
                scaled[s, o, g * 16 + j] = v[s, g * 16 + j].astype(F32) * column
            return carry

        lax.fori_loop(0, OCC // 16, body, 0)

    def slots(owner_y, i):
        t = (owner_y * 2 + core) * TPO + i
        return slot[0, t // 128, t % 128], slot[1, t // 128, t % 128]

    def local(s, owner_y, i):
        k0, k1 = slots(owner_y, i)
        return scaled[s, 0, k0] + scaled[s, 1, k1]

    def owner_of(way, h, n):
        away = n - h + 1
        return (y + away) % NY if way == RIGHT else (y + NY - away) % NY

    ring, totals = {}, {}

    def emit(s, way, half, h):
        n = hops(way, half)
        owner = owner_of(way, h, n)
        if h > 1:
            ring[s, way, half, h - 1].wait_recv()

        def body(g, carry):
            for j in range(4):
                i = g * 4 + j
                acc = local(s, owner, half * HALF + i)
                if h > 1:
                    acc = acc + recv[s, way, half, h - 2, i].astype(F32)
                send[s, way, half, h - 1, i] = acc.astype(BF16)
            return carry

        lax.fori_loop(0, HALF // 4, body, 0)
        copy = remote(
            send.at[s, way, half, h - 1], recv.at[s, way, half, h - 1],
            s_ring_s.at[s, way, half, h - 1], s_ring_r.at[s, way, half, h - 1], beside[way],
        )
        copy.start()
        ring[s, way, half, h] = copy

    def local_totals(owner):
        rows = pl.ds(pl.multiple_of((owner * 2 + core) * TPO, TPO), TPO)
        return tile_totals[0, rows, :] + tile_totals[1, rows, :]

    def emit_total(way, h):
        n = hops(way, 0)
        acc = local_totals(owner_of(way, h, n))
        if h > 1:
            totals[way, h - 1].wait_recv()
            acc = acc + trecv[way, h - 2].astype(F32)
        tsend[way, h - 1] = acc.astype(BF16)
        copy = remote(
            tsend.at[way, h - 1], trecv.at[way, h - 1], s_tot_s.at[way, h - 1], s_tot_r.at[way, h - 1], beside[way]
        )
        copy.start()
        totals[way, h] = copy

    def total_inverse():
        acc = local_totals(y)
        for way in (RIGHT, LEFT):
            n = hops(way, 0)
            totals[way, n].wait_recv()
            acc = acc + trecv[way, n - 1].astype(F32)
        rinv[0:TPO, :] = 1.0 / jnp.maximum(acc, 1.0)
        rinv[...] = rinv[...].T

    sends = []

    def finish(s):
        factor = rinv[pl.ds(s * ROWS, ROWS), :]
        for half in range(2):
            for way in (RIGHT, LEFT):
                ring[s, way, half, hops(way, half)].wait_recv()
            for j in range(HALF):
                i = half * HALF + j
                acc = local(s, y, i)
                for way in (RIGHT, LEFT):
                    acc = acc + recv[s, way, half, hops(way, half) - 1, j].astype(F32)
                norm[i] = acc * jnp.broadcast_to(factor[:, i : i + 1], (ROWS, 128))

        for c in range(CPP):
            blocks = [norm[i, c * 8 : (c + 1) * 8, :] for i in range(TPO)]
            for g, block in enumerate(block_transpose(blocks, 8, 1)):
                mixed[g, c] = block
        for g in range(16):
            parts = block_transpose([mixed[g, c] for c in range(CPP)], 2, 0)
            for lh in range(2):
                outbox[s, lh * 16 + g] = jnp.concatenate([parts[lh], parts[2 + lh]], 0).astype(BF16)

        def post(d, carry):
            to = peer(d)
            remote(outbox.at[s, to], inbox.at[s, ch], s_a2a_s.at[s], s_a2a_r.at[s], (ob, to)).start()
            return carry

        lax.fori_loop(1, NCH, post, 0)
        inbox[s, ch] = outbox[s, ch]

    def all_of(box, s, sem):
        some = box.at[s, pl.ds(0, NCH - 1)]
        return pltpu.make_async_copy(some, some, sem)

    def transform(s):
        all_of(inbox, s, s_a2a_r.at[s]).wait()
        if s == 0:
            load_tab.wait()
        cells = inbox[s].astype(F32).reshape(NCH, 2, 8, 128)
        for p in range(2):
            left = cells[:, p].reshape(NCH * 8, 128).T.astype(BF16)
            for b in range(2):
                right = jnp.concatenate([tabv[s, 3 * b + j] for j in range(3)], 1)
                block = jnp.dot(left, right, preferred_element_type=F32).reshape(TPO, 8, NCHAN)
                out[:, p, b] = block if s == 0 else out[:, p, b] + block

    for tick in range(PARTS + 4):
        if tick < PARTS:
            load[tick].wait()
            scale(tick, 0)
            if tick == 0:
                smalls[0].wait_recv()
                to_smem[1].start()
                smalls[1].wait_recv()
                roll_weights(1)
                for copy in to_smem:
                    copy.wait()
            swaps[tick].wait_recv()
            scale(tick, 1)
            if tick == 0:
                smalls[2].wait_recv()
        for h in range(1, 5):
            s = tick - h + 1
            if 0 <= s < PARTS:
                for half in range(2):
                    for way in (RIGHT, LEFT):
                        if h <= hops(way, half):
                            emit(s, way, half, h)
                if s == 0:
                    for way in (RIGHT, LEFT):
                        if h <= hops(way, 0):
                            emit_total(way, h)
        if tick == 4:
            total_inverse()
        if tick >= 4:
            finish(tick - 4)
        if tick >= 5:
            transform(tick - 5)
    transform(PARTS - 1)

    for copy in [*swaps, *smalls, *ring.values(), *totals.values()]:
        copy.wait_send()
    for s in range(PARTS):
        all_of(outbox, s, s_a2a_s.at[s]).wait()


def shards(visibilities, weights, coverage, owner_map):
    vis = visibilities.reshape(OCC, LOCAL, 2, 2, 2, 128).transpose(0, 1, 2, 4, 3, 5).reshape(OCC, LOCAL * 8, 128)
    weights = weights[0].transpose(1, 2, 0)
    owner_map = owner_map.reshape(2, 128)
    table = jnp.asarray(delay_table())

    vmem, hbm = (pl.BlockSpec(memory_space=m) for m in (pltpu.VMEM, pltpu.HBM))
    dma = pltpu.SemaphoreType.DMA
    return pl.pallas_call(
        kernel,
        out_shape=jax.ShapeDtypeStruct((TPO, 2, 2, 8, NCHAN), F32),
        in_specs=[hbm, vmem, vmem, vmem, hbm],
        out_specs=vmem,
        scratch_shapes=[
            pltpu.VMEM((PARTS, OCC, ROWS, 128), BF16),
            pltpu.VMEM((PARTS, OCC, ROWS, 128), BF16),
            pltpu.VMEM((2, 128, 128), F32),
            pltpu.VMEM((2, 4, 128, 128), F32),
            pltpu.VMEM((2, 2, 128), I32),
            pltpu.SMEM((2, 2, 128), I32),
            pltpu.VMEM((2, 2 * 128, 128), F32),
            pltpu.VMEM((PARTS, 2, OCC + 1, ROWS, 128), F32),
            pltpu.VMEM((2, 4, TPO, 128), BF16),
            pltpu.VMEM((2, 4, TPO, 128), BF16),
            pltpu.VMEM((128, 128), F32),
            pltpu.VMEM((PARTS, 2, 2, 4, HALF, ROWS, 128), BF16),
            pltpu.VMEM((PARTS, 2, 2, 4, HALF, ROWS, 128), BF16),
            pltpu.VMEM((TPO, ROWS, 128), F32),
            pltpu.VMEM((16, CPP, 8, 128), F32),
            pltpu.VMEM((PARTS, NCH, 16, 128), BF16),
            pltpu.VMEM((PARTS, NCH, 16, 128), BF16),
            pltpu.VMEM(table.shape, BF16),
            dma((PARTS,)),
            dma,
            dma((2,)),
            dma((PARTS,)),
            dma((PARTS,)),
            dma((3,)),
            dma((3,)),
            dma((2, 4)),
            dma((2, 4)),
            dma((PARTS, 2, 2, 4)),
            dma((PARTS, 2, 2, 4)),
            dma((PARTS,)),
            dma((PARTS,)),
        ],
        compiler_params=pltpu.CompilerParams(
            collective_id=0, has_side_effects=True, vmem_limit_bytes=62 * 1024 * 1024
        ),
    )(vis, weights, coverage, owner_map, table)


def solution(mesh):
    return jax.shard_map(
        shards,
        mesh=mesh,
        in_specs=(
            P("obs", None, "chan", None, None, None),
            P("obs", None, "chan", None),
            P("obs", None),
            P(),
        ),
        out_specs=P("obs", None, None, "chan", None),
        check_vma=False,
    )
```

```python
import functools
import math

import jax
import jax.numpy as jnp
import ml_dtypes
import numpy as np
from jax import lax
from jax.experimental import pallas as pl
from jax.experimental.pallas import tpu as pltpu
from jax.sharding import PartitionSpec as P

F32, BF16, I32 = jnp.float32, jnp.bfloat16, jnp.int32
MESH = pl.DeviceIdType.MESH

NCHAN = 384
OCC = 64
TPO = 16
CAP = 6
NX, NY, NZ = 4, 8, 8
NCH = NX * NZ
LOCAL = NCHAN // NCH
PARTS = 6
ROWS = LOCAL * 8 // PARTS
GROUPS = 3
CPG = LOCAL // GROUPS
LONG, SHORT = 0, 1
FIRST, SECOND, HOP, LAST = 0.0, 0.0, 2.0, 2.0
SLOT, SLOT1, ENTRY, RANKS, LISTS, RANK = 0, 1, 2, 3, 7, 7


def hops(chain):
    return 4 if chain == LONG else 3


def delay_table():
    n = np.arange(NCHAN)
    angle = 2.0 * math.pi * (np.outer(n, n) % NCHAN) / NCHAN
    base = 2.0 * math.pi * n / (NCHAN - 1)
    taper = 0.35875 - 0.48829 * np.cos(base) + 0.14128 * np.cos(2 * base) - 0.01168 * np.cos(3 * base)
    column = (taper / math.sqrt(NCHAN))[:, None]
    cosine, sine = column * np.cos(angle), column * np.sin(angle)
    table = np.stack([np.stack([cosine, -sine], 1), np.stack([sine, cosine], 1)], 0)
    table = table.astype(np.float32).astype(ml_dtypes.bfloat16)
    table = table.reshape(2, NCH, GROUPS, CPG, 2 * NCHAN).transpose(2, 1, 3, 0, 4)
    table = table.reshape(GROUPS, NCH * CPG * 2, 2 * NCHAN // 128, 128)
    return table.transpose(0, 2, 1, 3)


def swap(lo, hi, mask, shift, axis):
    size = lo.shape[axis]
    new_lo = jnp.where(mask, pltpu.roll(hi, shift, axis), lo)
    new_hi = jnp.where(mask, hi, pltpu.roll(lo, size - shift, axis))
    return new_lo, new_hi


def block_transpose(blocks, unit, axis):
    blocks = list(blocks)
    group = lax.broadcasted_iota(I32, blocks[0].shape, axis) // unit
    step = 1
    while step < len(blocks):
        mask = (group // step) % 2 == 1
        for i in range(len(blocks)):
            if (i // step) % 2 == 0:
                blocks[i], blocks[i + step] = swap(blocks[i], blocks[i + step], mask, unit * step, axis)
        step *= 2
    return blocks


def kernel(
    vis, weights, coverage, owner_map, tab, out,
    v0, v1, rw, counts, count_at, lists, listed_at, tile_totals, scaled, square, rinv, send1, recv1, got, send, recv, tsend, trecv,
    norm, mixed, outbox, inbox, tabv,
    s_v0, s_tab, s_counts, s_lists, s_sib_s, s_sib_r, s_small_s, s_small_r, s_rank_s, s_rank_r,
    s_one_s, s_one_r, s_ring_s, s_ring_r, s_tot_s, s_tot_r, s_a2a_s, s_a2a_r,
):
    ob = lax.axis_index("obs")
    ch = lax.axis_index("chan")
    y, core = ob // 2, ob % 2
    x, z = ch // NZ, ch % NZ
    sibling = (y * 2 + 1 - core, ch)
    above, below = (y + 1) % NY, (y + NY - 1) % NY

    def along(chain, parity, distance):
        sign = 1 - 2 * parity if chain == LONG else 2 * parity - 1
        return (y + NY + distance * sign) % NY

    def peer(d):
        return ((x + d // NZ) % NX) * NZ + (z + d % NZ) % NZ

    barrier = pltpu.get_barrier_semaphore()
    for device in [(near * 2 + c, ch) for near in (above, below) for c in range(2)] + [sibling]:
        pl.semaphore_signal(barrier, inc=1, device_id=device, device_id_type=MESH)

    def greet(d, carry):
        pl.semaphore_signal(barrier, inc=1, device_id=(ob, peer(d)), device_id_type=MESH)
        return carry

    lax.fori_loop(1, NCH, greet, 0)

    def part_of(ref, s):
        return ref.at[:, pl.ds(s * ROWS, ROWS), :]

    load = [pltpu.make_async_copy(part_of(vis, s), v0.at[s], s_v0.at[s]) for s in range(PARTS)]
    load_tab = pltpu.make_async_copy(tab, tabv, s_tab)
    for copy in load:
        copy.start()
    load_tab.start()

    rw[...] = jnp.zeros((128, 128), F32)
    first = lax.broadcasted_iota(I32, (8, OCC), 0) < 4
    for c in range(LOCAL):
        pair = weights[c].astype(F32)
        counts[0, c, :, 0:OCC] = pair
        rw[c * 8 : (c + 1) * 8, 0:OCC] = jnp.where(first, pair[0:1], pair[1:2])

    to_scalars = [pltpu.make_async_copy(counts.at[o], count_at.at[o], s_counts.at[o]) for o in range(2)]
    to_scalars[0].start()

    square[...] = jnp.zeros((128, 128), F32)
    square[:, 0:OCC] = jnp.broadcast_to(coverage[...].astype(F32), (128, OCC))
    number = square[...].T
    k = lax.broadcasted_iota(I32, (128, 128), 0)
    lane = lax.broadcasted_iota(I32, (128, 128), 1)
    same = [(number == owner_map[h : h + 1, :].astype(F32)) & (k < OCC) for h in range(2)]
    owner = sum(
        jnp.sum(jnp.where(same[h], ((lane + 128 * h) // TPO).astype(F32), 0.0), axis=1, keepdims=True) for h in range(2)
    )
    owner = jnp.broadcast_to(owner, (128, 128))
    earlier = (owner == owner.T) & (lane < k)
    rank = jnp.sum(jnp.where(earlier, 1.0, 0.0), axis=1, keepdims=True)
    rank = jnp.broadcast_to(jnp.minimum(rank, CAP * 1.0), (128, 128))
    for h in range(2):
        slot = jnp.min(jnp.where(same[h], k, OCC), axis=0, keepdims=True)
        before = (owner == ((lane + 128 * h) // TPO).astype(F32)) & (k < slot)
        count = jnp.minimum(jnp.sum(jnp.where(before, 1, 0), axis=0, keepdims=True), CAP)
        lists[SLOT, h : h + 1, :] = slot
        lists[RANK, h : h + 1, :] = jnp.where(slot < OCC, count, CAP)
    entry = owner * CAP + rank
    lists[ENTRY, 0:1, :] = jnp.min(
        jnp.where((entry == lane.astype(F32)) & (rank < CAP) & (k < OCC), k, OCC), axis=0, keepdims=True
    )
    lists[ENTRY, 1:2, :] = jnp.full((1, 128), OCC, I32)
    to_smem = [pltpu.make_async_copy(lists.at[i], listed_at.at[i], s_lists.at[i]) for i in range(LISTS)]
    to_smem[ENTRY].start()
    to_smem[SLOT].start()

    for s in range(PARTS):
        for o in range(2):
            scaled[s, o, OCC] = jnp.zeros((ROWS, 128), F32)
    for c in range(2):
        got[c, CAP] = jnp.zeros((ROWS, 128), F32)

    upper = lax.broadcasted_iota(I32, (8, 128), 0) < 4

    def scale(s, o):
        v = (v0, v1)[o]

        def body(g, carry):
            for j in range(8):
                k = g * 8 + j
                values = v[s, k].astype(F32)
                for c in range(2):
                    weight = jnp.where(upper, count_at[o, s * 2 + c, 0, k], count_at[o, s * 2 + c, 1, k])
                    scaled[s, o, k, c * 8 : c * 8 + 8] = values[c * 8 : c * 8 + 8] * weight
            return carry

        lax.fori_loop(0, OCC // 8, body, 0)

    def remote(src, dst, s_sem, r_sem, device):
        return pltpu.make_async_remote_copy(
            src_ref=src, dst_ref=dst, send_sem=s_sem, recv_sem=r_sem, device_id=device, device_id_type=MESH
        )

    sent = []

    def launch(copy):
        copy.start()
        sent.append(copy)
        return copy

    def arrived(ref, sem):
        pltpu.make_async_copy(ref, ref, sem).wait()

    def pack_first(s):
        for parity in range(2):
            for chain in (LONG, SHORT):
                base = (along(chain, parity, hops(chain)) * 2 + parity) * CAP
                for e in range(CAP):
                    send1[s, parity, chain, e] = scaled[s, 0, listed_at[ENTRY, 0, base + e]].astype(BF16)

    def send_first(s):
        for parity in range(2):
            for chain in (LONG, SHORT):
                launch(remote(
                    send1.at[s, parity, chain], recv1.at[s, chain, core],
                    s_one_s.at[s, parity, chain], s_one_r.at[s, chain, core],
                    (along(chain, parity, 1) * 2 + parity, ch),
                ))

    load[0].wait()
    to_scalars[0].wait()
    scale(0, 0)
    to_smem[ENTRY].wait()
    pack_first(0)

    for h in range(2):
        totals_t = jnp.dot(rw[...].astype(BF16), same[h].astype(F32).astype(BF16), preferred_element_type=F32)
        tile_totals[0, pl.ds(h * 128, 128), :] = totals_t.T

    pl.semaphore_wait(barrier, NCH + 4)

    smalls = [
        remote(src, dst, s_small_s.at[i], s_small_r.at[i], sibling)
        for i, (src, dst) in enumerate(
            ((lists.at[SLOT], lists.at[SLOT1]), (counts.at[0], counts.at[1]), (tile_totals.at[0], tile_totals.at[1]))
        )
    ]
    swaps = [remote(part_of(vis, s), v1.at[s], s_sib_s.at[s], s_sib_r.at[s], sibling) for s in range(PARTS)]
    send_first(0)
    launch(smalls[0])
    launch(smalls[1])
    launch(swaps[0])
    for side, near in ((0, above), (1, below)):
        for c in range(2):
            launch(remote(
                lists.at[RANK], lists.at[RANKS + side * 2 + core], s_rank_s.at[side, c], s_rank_r.at[side, core],
                (near * 2 + c, ch),
            ))
    launch(smalls[2])
    for copy in swaps[1:]:
        launch(copy)

    def local(s, tile):
        return scaled[s, 0, listed_at[SLOT, tile // 128, tile % 128]] + scaled[s, 1, listed_at[SLOT1, tile // 128, tile % 128]]

    ring, totals = {}, {}

    def emit(s, chain, h):
        owner_tiles = (along(chain, core, hops(chain) - h + 1) * 2 + core) * TPO
        if h > 2:
            ring[s, chain, h - 1].wait_recv()
        else:
            for c in range(2):
                arrived(recv1.at[s, chain, c], s_one_r.at[s, chain, c])
                got[c, 0:CAP] = recv1[s, chain, c].astype(F32)
        side = core if chain == LONG else 1 - core

        def body(g, carry):
            for j in range(8):
                i = g * 8 + j
                tile = owner_tiles + i
                acc = local(s, tile)
                if h > 2:
                    acc = acc + recv[s, chain, h - 3, i].astype(F32)
                else:
                    for c in range(2):
                        at = listed_at[RANKS + side * 2 + c, tile // 128, tile % 128]
                        acc = acc + got[c, at]
                send[s, chain, h - 2, i] = acc.astype(BF16)
            return carry

        lax.fori_loop(0, TPO // 8, body, 0)
        ring[s, chain, h] = launch(remote(
            send.at[s, chain, h - 2], recv.at[s, chain, h - 2],
            s_ring_s.at[s, chain, h - 2], s_ring_r.at[s, chain, h - 2], (along(chain, core, 1) * 2 + core, ch),
        ))

    def local_totals(owner_y):
        rows = pl.ds(pl.multiple_of((owner_y * 2 + core) * TPO, TPO), TPO)
        return tile_totals[0, rows, :] + tile_totals[1, rows, :]

    def emit_total(chain, h):
        acc = local_totals(along(chain, core, hops(chain) - h + 1))
        if h > 1:
            totals[chain, h - 1].wait_recv()
            acc = acc + trecv[chain, h - 2].astype(F32)
        tsend[chain, h - 1] = acc.astype(BF16)
        totals[chain, h] = launch(remote(
            tsend.at[chain, h - 1], trecv.at[chain, h - 1], s_tot_s.at[chain, h - 1], s_tot_r.at[chain, h - 1],
            (along(chain, core, 1) * 2 + core, ch),
        ))

    def total_inverse():
        acc = local_totals(y)
        for chain in (LONG, SHORT):
            totals[chain, hops(chain)].wait_recv()
            acc = acc + trecv[chain, hops(chain) - 1].astype(F32)
        square[0:TPO, :] = 1.0 / jnp.maximum(acc, 1.0)
        rinv[...] = square[...].T

    def settle(s):
        for chain in (LONG, SHORT):
            ring[s, chain, hops(chain)].wait_recv()
        factor = rinv[pl.ds(s * ROWS, ROWS), :]
        for i in range(TPO):
            acc = local(s, (y * 2 + core) * TPO + i)
            for chain in (LONG, SHORT):
                acc = acc + recv[s, chain, hops(chain) - 2, i].astype(F32)
            norm[i, s % 2] = acc * jnp.broadcast_to(factor[:, i : i + 1], (ROWS, 128))

    def exchange(g):
        for c in range(4):
            blocks = [norm[i, c // 2, (c % 2) * 8 : (c % 2) * 8 + 8, :] for i in range(TPO)]
            for group, block in enumerate(block_transpose(blocks, 8, 1)):
                mixed[group, c] = block
        for d in range(16):
            group = (ch + d) % 16
            parts = block_transpose([mixed[group, c] for c in range(4)], 2, 0)
            for lh in range(2):
                outbox[g, lh * 16 + group] = jnp.concatenate([parts[lh], parts[2 + lh]], 0).astype(BF16)
            for to in (group, 16 + group) if d else ((ch + 16) % NCH,):
                remote(outbox.at[g, to], inbox.at[g, ch], s_a2a_s.at[g], s_a2a_r.at[g], (ob, to)).start()
        inbox[g, ch] = outbox[g, ch]

    def transform(g):
        arrived(inbox.at[g, pl.ds(0, NCH - 1)], s_a2a_r.at[g])
        if g == 0:
            load_tab.wait()
        cells = inbox[g].astype(F32).reshape(NCH, 2, 8, 128)
        for p in range(2):
            left = cells[:, p].reshape(NCH * 8, 128).T.astype(BF16)
            for b in range(2):
                right = jnp.concatenate([tabv[g, 3 * b + j] for j in range(3)], 1)
                block = jnp.dot(left, right, preferred_element_type=F32).reshape(TPO, 8, NCHAN)
                out[:, p, b] = block if g == 0 else out[:, p, b] + block

    def first(s):
        if s:
            load[s].wait()
            scale(s, 0)
            pack_first(s)
            send_first(s)

    def second(s):
        if s == 0:
            smalls[0].wait_recv()
            to_smem[SLOT1].start()
            smalls[1].wait_recv()
            to_scalars[1].start()
            for side in range(2):
                for c in range(2):
                    arrived(lists.at[RANKS + side * 2 + c], s_rank_r.at[side, c])
                    to_smem[RANKS + side * 2 + c].start()
            for i in range(LISTS):
                if i != ENTRY:
                    to_smem[i].wait()
            to_scalars[1].wait()
        swaps[s].wait_recv()
        scale(s, 1)

    def hop(s, h):
        for chain in (LONG, SHORT):
            if h <= hops(chain):
                emit(s, chain, h)
        if s == 0:
            if h == 2:
                smalls[2].wait_recv()
                emit_total(LONG, 1)
                emit_total(SHORT, 1)
            for chain in (LONG, SHORT):
                if h <= hops(chain):
                    emit_total(chain, h)

    def last(s):
        if s == 0:
            total_inverse()
        settle(s)
        if s % 2:
            exchange(s // 2)

    steps = []
    for s in range(PARTS):
        steps.append((FIRST * s, 0, s, first, (s,)))
        steps.append((s + HOP - SECOND, 1, s, second, (s,)))
        for h in range(2, 5):
            steps.append((s + HOP * (h - 1), h, s, hop, (s, h)))
        steps.append((s + HOP * 3 + LAST, 5, s, last, (s,)))
    for *_, step, which in sorted(steps, key=lambda step: step[:3]):
        step(*which)
    for g in range(GROUPS):
        transform(g)

    for copy in sent:
        copy.wait_send()
    for g in range(GROUPS):
        arrived(outbox.at[g, pl.ds(0, NCH - 1)], s_a2a_s.at[g])


def shards(visibilities, weights, coverage, owner_map):
    vis = visibilities.reshape(OCC, LOCAL, 2, 2, 2, 128).transpose(0, 1, 2, 4, 3, 5).reshape(OCC, LOCAL * 8, 128)
    weights = weights[0].transpose(1, 2, 0)
    owner_map = owner_map.reshape(2, 128)
    table = jnp.asarray(delay_table())

    vmem, hbm = (pl.BlockSpec(memory_space=m) for m in (pltpu.VMEM, pltpu.HBM))
    dma = pltpu.SemaphoreType.DMA
    return pl.pallas_call(
        kernel,
        out_shape=jax.ShapeDtypeStruct((TPO, 2, 2, 8, NCHAN), F32),
        in_specs=[hbm, vmem, vmem, vmem, hbm],
        out_specs=vmem,
        scratch_shapes=[
            pltpu.VMEM((PARTS, OCC, ROWS, 128), BF16),
            pltpu.VMEM((PARTS, OCC, ROWS, 128), BF16),
            pltpu.VMEM((128, 128), F32),
            pltpu.VMEM((2, LOCAL, 2, 128), F32),
            pltpu.SMEM((2, LOCAL, 2, 128), F32),
            pltpu.VMEM((LISTS + 1, 2, 128), I32),
            pltpu.SMEM((LISTS, 2, 128), I32),
            pltpu.VMEM((2, 2 * 128, 128), F32),
            pltpu.VMEM((PARTS, 2, OCC + 1, ROWS, 128), F32),
            pltpu.VMEM((128, 128), F32),
            pltpu.VMEM((128, 128), F32),
            pltpu.VMEM((PARTS, 2, 2, CAP, ROWS, 128), BF16),
            pltpu.VMEM((PARTS, 2, 2, CAP, ROWS, 128), BF16),
            pltpu.VMEM((2, CAP + 1, ROWS, 128), F32),
            pltpu.VMEM((PARTS, 2, 3, TPO, ROWS, 128), BF16),
            pltpu.VMEM((PARTS, 2, 3, TPO, ROWS, 128), BF16),
            pltpu.VMEM((2, 4, TPO, 128), BF16),
            pltpu.VMEM((2, 4, TPO, 128), BF16),
            pltpu.VMEM((TPO, 2, ROWS, 128), F32),
            pltpu.VMEM((16, CPG, 8, 128), F32),
            pltpu.VMEM((GROUPS, NCH, 16, 128), BF16),
            pltpu.VMEM((GROUPS, NCH, 16, 128), BF16),
            pltpu.VMEM(table.shape, BF16),
            dma((PARTS,)),
            dma,
            dma((2,)),
            dma((LISTS,)),
            dma((PARTS,)),
            dma((PARTS,)),
            dma((3,)),
            dma((3,)),
            dma((2, 2)),
            dma((2, 2)),
            dma((PARTS, 2, 2)),
            dma((PARTS, 2, 2)),
            dma((PARTS, 2, 3)),
            dma((PARTS, 2, 3)),
            dma((2, 4)),
            dma((2, 4)),
            dma((GROUPS,)),
            dma((GROUPS,)),
        ],
        compiler_params=pltpu.CompilerParams(
            collective_id=0, has_side_effects=True, vmem_limit_bytes=60 * 1024 * 1024
        ),
    )(vis, weights, coverage, owner_map, table)


def solution(mesh):
    return jax.shard_map(
        shards,
        mesh=mesh,
        in_specs=(
            P("obs", None, "chan", None, None, None),
            P("obs", None, "chan", None),
            P("obs", None),
            P(),
        ),
        out_specs=P("obs", None, None, "chan", None),
        check_vma=False,
    )
```

```python
import functools
import math

import jax
import jax.numpy as jnp
import ml_dtypes
import numpy as np
from jax import lax
from jax.experimental import pallas as pl
from jax.experimental.pallas import tpu as pltpu
from jax.sharding import PartitionSpec as P

F32, BF16, I32 = jnp.float32, jnp.bfloat16, jnp.int32
MESH = pl.DeviceIdType.MESH

NCHAN = 384
OCC = 64
TPO = 16
CAP = 6
NX, NY, NZ = 4, 8, 8
NCH = NX * NZ
LOCAL = NCHAN // NCH
PARTS = 6
ROWS = LOCAL * 8 // PARTS
GROUPS = 3
CPG = LOCAL // GROUPS
LONG, SHORT = 0, 1
FAR_FIRST = (4, 12, 3, 11, 5, 13, 2, 10, 6, 14, 1, 9, 7, 15, 8, 0)
FIRST, SECOND, HOP, LAST = 0.0, 0.0, 2.0, 2.0
SLOT, SLOT1, ENTRY, RANKS, LISTS, RANK = 0, 1, 2, 3, 7, 7


def hops(chain):
    return 4 if chain == LONG else 3


def delay_table():
    n = np.arange(NCHAN)
    angle = 2.0 * math.pi * (np.outer(n, n) % NCHAN) / NCHAN
    base = 2.0 * math.pi * n / (NCHAN - 1)
    taper = 0.35875 - 0.48829 * np.cos(base) + 0.14128 * np.cos(2 * base) - 0.01168 * np.cos(3 * base)
    column = (taper / math.sqrt(NCHAN))[:, None]
    cosine, sine = column * np.cos(angle), column * np.sin(angle)
    table = np.stack([np.stack([cosine, -sine], 1), np.stack([sine, cosine], 1)], 0)
    table = table.astype(np.float32).astype(ml_dtypes.bfloat16)
    table = table.reshape(2, NCH, GROUPS, CPG, 2 * NCHAN).transpose(2, 1, 3, 0, 4)
    table = table.reshape(GROUPS, NCH * CPG * 2, 2 * NCHAN // 128, 128)
    return table.transpose(0, 2, 1, 3)


def swap(lo, hi, mask, shift, axis):
    size = lo.shape[axis]
    new_lo = jnp.where(mask, pltpu.roll(hi, shift, axis), lo)
    new_hi = jnp.where(mask, hi, pltpu.roll(lo, size - shift, axis))
    return new_lo, new_hi


def block_transpose(blocks, unit, axis):
    blocks = list(blocks)
    group = lax.broadcasted_iota(I32, blocks[0].shape, axis) // unit
    step = 1
    while step < len(blocks):
        mask = (group // step) % 2 == 1
        for i in range(len(blocks)):
            if (i // step) % 2 == 0:
                blocks[i], blocks[i + step] = swap(blocks[i], blocks[i + step], mask, unit * step, axis)
        step *= 2
    return blocks


def kernel(
    vis, weights, coverage, owner_map, tab, out,
    v0, v1, rw, counts, count_at, lists, listed_at, tile_totals, scaled, square, rinv, send1, recv1, got, send, recv, tsend, trecv,
    norm, mixed, outbox, inbox, tabv,
    s_v0, s_tab, s_counts, s_lists, s_sib_s, s_sib_r, s_small_s, s_small_r, s_rank_s, s_rank_r,
    s_one_s, s_one_r, s_ring_s, s_ring_r, s_tot_s, s_tot_r, s_a2a_s, s_a2a_r,
):
    ob = lax.axis_index("obs")
    ch = lax.axis_index("chan")
    y, core = ob // 2, ob % 2
    x, z = ch // NZ, ch % NZ
    sibling = (y * 2 + 1 - core, ch)
    above, below = (y + 1) % NY, (y + NY - 1) % NY

    def along(chain, parity, distance):
        sign = 1 - 2 * parity if chain == LONG else 2 * parity - 1
        return (y + NY + distance * sign) % NY

    def peer(d):
        return ((x + d // NZ) % NX) * NZ + (z + d % NZ) % NZ

    barrier = pltpu.get_barrier_semaphore()
    for device in [(near * 2 + c, ch) for near in (above, below) for c in range(2)] + [sibling]:
        pl.semaphore_signal(barrier, inc=1, device_id=device, device_id_type=MESH)

    def greet(d, carry):
        pl.semaphore_signal(barrier, inc=1, device_id=(ob, peer(d)), device_id_type=MESH)
        return carry

    lax.fori_loop(1, NCH, greet, 0)

    def part_of(ref, s):
        return ref.at[:, pl.ds(s * ROWS, ROWS), :]

    load = [pltpu.make_async_copy(part_of(vis, s), v0.at[s], s_v0.at[s]) for s in range(PARTS)]
    load_tab = pltpu.make_async_copy(tab, tabv, s_tab)
    for copy in load:
        copy.start()
    load_tab.start()

    rw[...] = jnp.zeros((128, 128), F32)
    first = lax.broadcasted_iota(I32, (8, OCC), 0) < 4
    for c in range(LOCAL):
        pair = weights[c].astype(F32)
        counts[0, c, :, 0:OCC] = pair
        rw[c * 8 : (c + 1) * 8, 0:OCC] = jnp.where(first, pair[0:1], pair[1:2])

    to_scalars = [pltpu.make_async_copy(counts.at[o], count_at.at[o], s_counts.at[o]) for o in range(2)]
    to_scalars[0].start()

    square[...] = jnp.zeros((128, 128), F32)
    square[:, 0:OCC] = jnp.broadcast_to(coverage[...].astype(F32), (128, OCC))
    number = square[...].T
    k = lax.broadcasted_iota(I32, (128, 128), 0)
    lane = lax.broadcasted_iota(I32, (128, 128), 1)
    same = [(number == owner_map[h : h + 1, :].astype(F32)) & (k < OCC) for h in range(2)]
    owner = sum(
        jnp.sum(jnp.where(same[h], ((lane + 128 * h) // TPO).astype(F32), 0.0), axis=1, keepdims=True) for h in range(2)
    )
    owner = jnp.broadcast_to(owner, (128, 128))
    earlier = (owner == owner.T) & (lane < k)
    rank = jnp.sum(jnp.where(earlier, 1.0, 0.0), axis=1, keepdims=True)
    rank = jnp.broadcast_to(jnp.minimum(rank, CAP * 1.0), (128, 128))
    for h in range(2):
        slot = jnp.min(jnp.where(same[h], k, OCC), axis=0, keepdims=True)
        before = (owner == ((lane + 128 * h) // TPO).astype(F32)) & (k < slot)
        count = jnp.minimum(jnp.sum(jnp.where(before, 1, 0), axis=0, keepdims=True), CAP)
        lists[SLOT, h : h + 1, :] = slot
        lists[RANK, h : h + 1, :] = jnp.where(slot < OCC, count, CAP)
    entry = owner * CAP + rank
    lists[ENTRY, 0:1, :] = jnp.min(
        jnp.where((entry == lane.astype(F32)) & (rank < CAP) & (k < OCC), k, OCC), axis=0, keepdims=True
    )
    lists[ENTRY, 1:2, :] = jnp.full((1, 128), OCC, I32)
    to_smem = [pltpu.make_async_copy(lists.at[i], listed_at.at[i], s_lists.at[i]) for i in range(LISTS)]
    to_smem[ENTRY].start()
    to_smem[SLOT].start()

    for s in range(PARTS):
        for o in range(2):
            scaled[s, o, OCC] = jnp.zeros((ROWS, 128), F32)
    for c in range(2):
        got[c, CAP] = jnp.zeros((ROWS, 128), F32)

    upper = lax.broadcasted_iota(I32, (8, 128), 0) < 4

    def scale(s, o):
        v = (v0, v1)[o]

        def body(g, carry):
            for j in range(8):
                k = g * 8 + j
                values = v[s, k].astype(F32)
                for c in range(2):
                    weight = jnp.where(upper, count_at[o, s * 2 + c, 0, k], count_at[o, s * 2 + c, 1, k])
                    scaled[s, o, k, c * 8 : c * 8 + 8] = values[c * 8 : c * 8 + 8] * weight
            return carry

        lax.fori_loop(0, OCC // 8, body, 0)

    def remote(src, dst, s_sem, r_sem, device):
        return pltpu.make_async_remote_copy(
            src_ref=src, dst_ref=dst, send_sem=s_sem, recv_sem=r_sem, device_id=device, device_id_type=MESH
        )

    sent = []

    def launch(copy):
        copy.start()
        sent.append(copy)
        return copy

    def arrived(ref, sem):
        pltpu.make_async_copy(ref, ref, sem).wait()

    def pack_first(s):
        for parity in range(2):
            for chain in (LONG, SHORT):
                base = (along(chain, parity, hops(chain)) * 2 + parity) * CAP
                for e in range(CAP):
                    send1[s, parity, chain, e] = scaled[s, 0, listed_at[ENTRY, 0, base + e]].astype(BF16)

    def send_first(s):
        for parity in range(2):
            for chain in (LONG, SHORT):
                launch(remote(
                    send1.at[s, parity, chain], recv1.at[s, chain, core],
                    s_one_s.at[s, parity, chain], s_one_r.at[s, chain, core],
                    (along(chain, parity, 1) * 2 + parity, ch),
                ))

    load[0].wait()
    to_scalars[0].wait()
    scale(0, 0)
    to_smem[ENTRY].wait()
    pack_first(0)

    for h in range(2):
        totals_t = jnp.dot(rw[...].astype(BF16), same[h].astype(F32).astype(BF16), preferred_element_type=F32)
        tile_totals[0, pl.ds(h * 128, 128), :] = totals_t.T

    pl.semaphore_wait(barrier, NCH + 4)

    smalls = [
        remote(src, dst, s_small_s.at[i], s_small_r.at[i], sibling)
        for i, (src, dst) in enumerate(
            ((lists.at[SLOT], lists.at[SLOT1]), (counts.at[0], counts.at[1]), (tile_totals.at[0], tile_totals.at[1]))
        )
    ]
    swaps = [remote(part_of(vis, s), v1.at[s], s_sib_s.at[s], s_sib_r.at[s], sibling) for s in range(PARTS)]
    send_first(0)
    launch(smalls[0])
    launch(smalls[1])
    launch(swaps[0])
    for side, near in ((0, above), (1, below)):
        for c in range(2):
            launch(remote(
                lists.at[RANK], lists.at[RANKS + side * 2 + core], s_rank_s.at[side, c], s_rank_r.at[side, core],
                (near * 2 + c, ch),
            ))
    launch(smalls[2])
    for copy in swaps[1:]:
        launch(copy)

    def local(s, tile):
        return scaled[s, 0, listed_at[SLOT, tile // 128, tile % 128]] + scaled[s, 1, listed_at[SLOT1, tile // 128, tile % 128]]

    ring, totals = {}, {}

    def emit(s, chain, h):
        owner_tiles = (along(chain, core, hops(chain) - h + 1) * 2 + core) * TPO
        if h > 2:
            ring[s, chain, h - 1].wait_recv()
        else:
            for c in range(2):
                arrived(recv1.at[s, chain, c], s_one_r.at[s, chain, c])
                got[c, 0:CAP] = recv1[s, chain, c].astype(F32)
        side = core if chain == LONG else 1 - core

        def body(g, carry):
            for j in range(8):
                i = g * 8 + j
                tile = owner_tiles + i
                acc = local(s, tile)
                if h > 2:
                    acc = acc + recv[s, chain, h - 3, i].astype(F32)
                else:
                    for c in range(2):
                        at = listed_at[RANKS + side * 2 + c, tile // 128, tile % 128]
                        acc = acc + got[c, at]
                send[s, chain, h - 2, i] = acc.astype(BF16)
            return carry

        lax.fori_loop(0, TPO // 8, body, 0)
        ring[s, chain, h] = launch(remote(
            send.at[s, chain, h - 2], recv.at[s, chain, h - 2],
            s_ring_s.at[s, chain, h - 2], s_ring_r.at[s, chain, h - 2], (along(chain, core, 1) * 2 + core, ch),
        ))

    def local_totals(owner_y):
        rows = pl.ds(pl.multiple_of((owner_y * 2 + core) * TPO, TPO), TPO)
        return tile_totals[0, rows, :] + tile_totals[1, rows, :]

    def emit_total(chain, h):
        acc = local_totals(along(chain, core, hops(chain) - h + 1))
        if h > 1:
            totals[chain, h - 1].wait_recv()
            acc = acc + trecv[chain, h - 2].astype(F32)
        tsend[chain, h - 1] = acc.astype(BF16)
        totals[chain, h] = launch(remote(
            tsend.at[chain, h - 1], trecv.at[chain, h - 1], s_tot_s.at[chain, h - 1], s_tot_r.at[chain, h - 1],
            (along(chain, core, 1) * 2 + core, ch),
        ))

    def total_inverse():
        acc = local_totals(y)
        for chain in (LONG, SHORT):
            totals[chain, hops(chain)].wait_recv()
            acc = acc + trecv[chain, hops(chain) - 1].astype(F32)
        square[0:TPO, :] = 1.0 / jnp.maximum(acc, 1.0)
        rinv[...] = square[...].T

    def settle(s):
        for chain in (LONG, SHORT):
            ring[s, chain, hops(chain)].wait_recv()
        factor = rinv[pl.ds(s * ROWS, ROWS), :]
        for i in range(TPO):
            acc = local(s, (y * 2 + core) * TPO + i)
            for chain in (LONG, SHORT):
                acc = acc + recv[s, chain, hops(chain) - 2, i].astype(F32)
            norm[i, s % 2] = acc * jnp.broadcast_to(factor[:, i : i + 1], (ROWS, 128))

    def exchange(g):
        for c in range(4):
            blocks = [norm[i, c // 2, (c % 2) * 8 : (c % 2) * 8 + 8, :] for i in range(TPO)]
            for group, block in enumerate(block_transpose(blocks, 8, 1)):
                mixed[group, c] = block
        for d in FAR_FIRST:
            group = (ch + d) % 16
            parts = block_transpose([mixed[group, c] for c in range(4)], 2, 0)
            for lh in range(2):
                outbox[g, lh * 16 + group] = jnp.concatenate([parts[lh], parts[2 + lh]], 0).astype(BF16)
            for to in (group, 16 + group) if d else ((ch + 16) % NCH,):
                remote(outbox.at[g, to], inbox.at[g, ch], s_a2a_s.at[g], s_a2a_r.at[g], (ob, to)).start()
        inbox[g, ch] = outbox[g, ch]

    def transform(g):
        arrived(inbox.at[g, pl.ds(0, NCH - 1)], s_a2a_r.at[g])
        if g == 0:
            load_tab.wait()
        cells = inbox[g].astype(F32).reshape(NCH, 2, 8, 128)
        for p in range(2):
            left = cells[:, p].reshape(NCH * 8, 128).T.astype(BF16)
            for b in range(2):
                right = jnp.concatenate([tabv[g, 3 * b + j] for j in range(3)], 1)
                block = jnp.dot(left, right, preferred_element_type=F32).reshape(TPO, 8, NCHAN)
                out[:, p, b] = block if g == 0 else out[:, p, b] + block

    def first(s):
        if s:
            load[s].wait()
            scale(s, 0)
            pack_first(s)
            send_first(s)

    def second(s):
        if s == 0:
            smalls[0].wait_recv()
            to_smem[SLOT1].start()
            smalls[1].wait_recv()
            to_scalars[1].start()
            for side in range(2):
                for c in range(2):
                    arrived(lists.at[RANKS + side * 2 + c], s_rank_r.at[side, c])
                    to_smem[RANKS + side * 2 + c].start()
            for i in range(LISTS):
                if i != ENTRY:
                    to_smem[i].wait()
            to_scalars[1].wait()
        swaps[s].wait_recv()
        scale(s, 1)

    def hop(s, h):
        for chain in (LONG, SHORT):
            if h <= hops(chain):
                emit(s, chain, h)
        if s == 0:
            if h == 2:
                smalls[2].wait_recv()
                emit_total(LONG, 1)
                emit_total(SHORT, 1)
            for chain in (LONG, SHORT):
                if h <= hops(chain):
                    emit_total(chain, h)

    def last(s):
        if s == 0:
            total_inverse()
        settle(s)
        if s % 2:
            exchange(s // 2)

    steps = []
    for s in range(PARTS):
        steps.append((FIRST * s, 0, s, first, (s,)))
        steps.append((s + HOP - SECOND, 1, s, second, (s,)))
        for h in range(2, 5):
            steps.append((s + HOP * (h - 1), h, s, hop, (s, h)))
        steps.append((s + HOP * 3 + LAST, 5, s, last, (s,)))
    for *_, step, which in sorted(steps, key=lambda step: step[:3]):
        step(*which)
    for g in range(GROUPS - 1):
        transform(g)
    for copy in sent:
        copy.wait_send()
    for g in range(GROUPS):
        arrived(outbox.at[g, pl.ds(0, NCH - 1)], s_a2a_s.at[g])
    transform(GROUPS - 1)


def shards(visibilities, weights, coverage, owner_map):
    vis = visibilities.reshape(OCC, LOCAL, 2, 2, 2, 128).transpose(0, 1, 2, 4, 3, 5).reshape(OCC, LOCAL * 8, 128)
    weights = weights[0].transpose(1, 2, 0)
    owner_map = owner_map.reshape(2, 128)
    table = jnp.asarray(delay_table())

    vmem, hbm = (pl.BlockSpec(memory_space=m) for m in (pltpu.VMEM, pltpu.HBM))
    dma = pltpu.SemaphoreType.DMA
    return pl.pallas_call(
        kernel,
        out_shape=jax.ShapeDtypeStruct((TPO, 2, 2, 8, NCHAN), F32),
        in_specs=[hbm, vmem, vmem, vmem, hbm],
        out_specs=vmem,
        scratch_shapes=[
            pltpu.VMEM((PARTS, OCC, ROWS, 128), BF16),
            pltpu.VMEM((PARTS, OCC, ROWS, 128), BF16),
            pltpu.VMEM((128, 128), F32),
            pltpu.VMEM((2, LOCAL, 2, 128), F32),
            pltpu.SMEM((2, LOCAL, 2, 128), F32),
            pltpu.VMEM((LISTS + 1, 2, 128), I32),
            pltpu.SMEM((LISTS, 2, 128), I32),
            pltpu.VMEM((2, 2 * 128, 128), F32),
            pltpu.VMEM((PARTS, 2, OCC + 1, ROWS, 128), F32),
            pltpu.VMEM((128, 128), F32),
            pltpu.VMEM((128, 128), F32),
            pltpu.VMEM((PARTS, 2, 2, CAP, ROWS, 128), BF16),
            pltpu.VMEM((PARTS, 2, 2, CAP, ROWS, 128), BF16),
            pltpu.VMEM((2, CAP + 1, ROWS, 128), F32),
            pltpu.VMEM((PARTS, 2, 3, TPO, ROWS, 128), BF16),
            pltpu.VMEM((PARTS, 2, 3, TPO, ROWS, 128), BF16),
            pltpu.VMEM((2, 4, TPO, 128), BF16),
            pltpu.VMEM((2, 4, TPO, 128), BF16),
            pltpu.VMEM((TPO, 2, ROWS, 128), F32),
            pltpu.VMEM((16, CPG, 8, 128), F32),
            pltpu.VMEM((GROUPS, NCH, 16, 128), BF16),
            pltpu.VMEM((GROUPS, NCH, 16, 128), BF16),
            pltpu.VMEM(table.shape, BF16),
            dma((PARTS,)),
            dma,
            dma((2,)),
            dma((LISTS,)),
            dma((PARTS,)),
            dma((PARTS,)),
            dma((3,)),
            dma((3,)),
            dma((2, 2)),
            dma((2, 2)),
            dma((PARTS, 2, 2)),
            dma((PARTS, 2, 2)),
            dma((PARTS, 2, 3)),
            dma((PARTS, 2, 3)),
            dma((2, 4)),
            dma((2, 4)),
            dma((GROUPS,)),
            dma((GROUPS,)),
        ],
        compiler_params=pltpu.CompilerParams(
            collective_id=0, has_side_effects=True, vmem_limit_bytes=53 * 1024 * 1024
        ),
    )(vis, weights, coverage, owner_map, table)


def solution(mesh):
    return jax.shard_map(
        shards,
        mesh=mesh,
        in_specs=(
            P("obs", None, "chan", None, None, None),
            P("obs", None, "chan", None),
            P("obs", None),
            P(),
        ),
        out_specs=P("obs", None, None, "chan", None),
        check_vma=False,
    )
```

```python
import functools
import math

import jax
import jax.numpy as jnp
import ml_dtypes
import numpy as np
from jax import lax
from jax.experimental import pallas as pl
from jax.experimental.pallas import tpu as pltpu
from jax.sharding import PartitionSpec as P

F32, BF16, I32 = jnp.float32, jnp.bfloat16, jnp.int32
MESH = pl.DeviceIdType.MESH

NCHAN = 384
OCC = 64
TPO = 16
CAP = 6
NX, NY, NZ = 4, 8, 8
NCH = NX * NZ
LOCAL = NCHAN // NCH
PARTS = 6
ROWS = LOCAL * 8 // PARTS
GROUPS = 3
CPG = LOCAL // GROUPS
LONG, SHORT = 0, 1
FAR_FIRST = (4, 12, 3, 11, 5, 13, 2, 10, 6, 14, 1, 9, 7, 15, 8, 0)
FIRST, SECOND, HOP, LAST = 0.0, 0.0, 2.0, 2.0
SLOT, SLOT1, ENTRY, RANKS, LISTS, RANK = 0, 1, 2, 3, 7, 7


def hops(chain):
    return 4 if chain == LONG else 3


def delay_table():
    n = np.arange(NCHAN)
    angle = 2.0 * math.pi * (np.outer(n, n) % NCHAN) / NCHAN
    base = 2.0 * math.pi * n / (NCHAN - 1)
    taper = 0.35875 - 0.48829 * np.cos(base) + 0.14128 * np.cos(2 * base) - 0.01168 * np.cos(3 * base)
    column = (taper / math.sqrt(NCHAN))[:, None]
    cosine, sine = column * np.cos(angle), column * np.sin(angle)
    table = np.stack([np.stack([cosine, -sine], 1), np.stack([sine, cosine], 1)], 0)
    table = table.astype(np.float32).astype(ml_dtypes.bfloat16)
    table = table.reshape(2, NCH, GROUPS, CPG, 2 * NCHAN).transpose(2, 1, 3, 0, 4)
    table = table.reshape(GROUPS, NCH * CPG * 2, 2 * NCHAN // 128, 128)
    return table.transpose(0, 2, 1, 3)


def swap(lo, hi, mask, shift, axis):
    size = lo.shape[axis]
    new_lo = jnp.where(mask, pltpu.roll(hi, shift, axis), lo)
    new_hi = jnp.where(mask, hi, pltpu.roll(lo, size - shift, axis))
    return new_lo, new_hi


def block_transpose(blocks, unit, axis):
    blocks = list(blocks)
    group = lax.broadcasted_iota(I32, blocks[0].shape, axis) // unit
    step = 1
    while step < len(blocks):
        mask = (group // step) % 2 == 1
        for i in range(len(blocks)):
            if (i // step) % 2 == 0:
                blocks[i], blocks[i + step] = swap(blocks[i], blocks[i + step], mask, unit * step, axis)
        step *= 2
    return blocks


def kernel(
    vis, small, tab, out,
    v0, v1, rw, counts, count_at, lists, listed_at, tile_totals, scaled, square, rinv, send1, recv1, got, send, recv, tsend, trecv,
    norm, mixed, outbox, inbox, tabv,
    s_v0, s_tab, s_counts, s_lists, s_sib_s, s_sib_r, s_small_s, s_small_r, s_rank_s, s_rank_r,
    s_one_s, s_one_r, s_ring_s, s_ring_r, s_tot_s, s_tot_r, s_a2a_s, s_a2a_r,
):
    ob = lax.axis_index("obs")
    ch = lax.axis_index("chan")
    y, core = ob // 2, ob % 2
    x, z = ch // NZ, ch % NZ
    sibling = (y * 2 + 1 - core, ch)
    above, below = (y + 1) % NY, (y + NY - 1) % NY

    def along(chain, parity, distance):
        sign = 1 - 2 * parity if chain == LONG else 2 * parity - 1
        return (y + NY + distance * sign) % NY

    def peer(d):
        return ((x + d // NZ) % NX) * NZ + (z + d % NZ) % NZ

    barrier = pltpu.get_barrier_semaphore()
    for device in [(near * 2 + c, ch) for near in (above, below) for c in range(2)] + [sibling]:
        pl.semaphore_signal(barrier, inc=1, device_id=device, device_id_type=MESH)

    def greet(d, carry):
        pl.semaphore_signal(barrier, inc=1, device_id=(ob, peer(d)), device_id_type=MESH)
        return carry

    lax.fori_loop(1, NCH, greet, 0)

    def part_of(ref, s):
        return ref.at[:, pl.ds(s * ROWS, ROWS), :]

    load = [pltpu.make_async_copy(part_of(vis, s), v0.at[s], s_v0.at[s]) for s in range(PARTS)]
    load_tab = pltpu.make_async_copy(tab, tabv, s_tab)
    for copy in load:
        copy.start()
    load_tab.start()

    rw[...] = jnp.zeros((128, 128), F32)
    first = lax.broadcasted_iota(I32, (8, OCC), 0) < 4
    for c in range(LOCAL):
        pair = small[2 * c : 2 * c + 2, 0:OCC].astype(F32)
        counts[0, c, :, 0:OCC] = pair
        rw[c * 8 : (c + 1) * 8, 0:OCC] = jnp.where(first, pair[0:1], pair[1:2])

    to_scalars = [pltpu.make_async_copy(counts.at[o], count_at.at[o], s_counts.at[o]) for o in range(2)]
    to_scalars[0].start()

    square[...] = jnp.zeros((128, 128), F32)
    square[:, 0:OCC] = jnp.broadcast_to(small[2 * LOCAL : 2 * LOCAL + 1, 0:OCC].astype(F32), (128, OCC))
    number = square[...].T
    k = lax.broadcasted_iota(I32, (128, 128), 0)
    lane = lax.broadcasted_iota(I32, (128, 128), 1)
    same = [(number == small[2 * LOCAL + 1 + h : 2 * LOCAL + 2 + h, :].astype(F32)) & (k < OCC) for h in range(2)]
    owner = sum(
        jnp.sum(jnp.where(same[h], ((lane + 128 * h) // TPO).astype(F32), 0.0), axis=1, keepdims=True) for h in range(2)
    )
    owner = jnp.broadcast_to(owner, (128, 128))
    earlier = (owner == owner.T) & (lane < k)
    rank = jnp.sum(jnp.where(earlier, 1.0, 0.0), axis=1, keepdims=True)
    rank = jnp.broadcast_to(jnp.minimum(rank, CAP * 1.0), (128, 128))
    for h in range(2):
        slot = jnp.min(jnp.where(same[h], k, OCC), axis=0, keepdims=True)
        before = (owner == ((lane + 128 * h) // TPO).astype(F32)) & (k < slot)
        count = jnp.minimum(jnp.sum(jnp.where(before, 1, 0), axis=0, keepdims=True), CAP)
        lists[SLOT, h : h + 1, :] = slot
        lists[RANK, h : h + 1, :] = jnp.where(slot < OCC, count, CAP)
    entry = owner * CAP + rank
    lists[ENTRY, 0:1, :] = jnp.min(
        jnp.where((entry == lane.astype(F32)) & (rank < CAP) & (k < OCC), k, OCC), axis=0, keepdims=True
    )
    lists[ENTRY, 1:2, :] = jnp.full((1, 128), OCC, I32)
    to_smem = [pltpu.make_async_copy(lists.at[i], listed_at.at[i], s_lists.at[i]) for i in range(LISTS)]
    to_smem[ENTRY].start()
    to_smem[SLOT].start()

    for s in range(PARTS):
        for o in range(2):
            scaled[s, o, OCC] = jnp.zeros((ROWS, 128), F32)
    for c in range(2):
        got[c, CAP] = jnp.zeros((ROWS, 128), F32)

    upper = lax.broadcasted_iota(I32, (8, 128), 0) < 4

    def scale(s, o):
        v = (v0, v1)[o]

        def body(g, carry):
            for j in range(8):
                k = g * 8 + j
                values = v[s, k].astype(F32)
                for c in range(2):
                    weight = jnp.where(upper, count_at[o, s * 2 + c, 0, k], count_at[o, s * 2 + c, 1, k])
                    scaled[s, o, k, c * 8 : c * 8 + 8] = values[c * 8 : c * 8 + 8] * weight
            return carry

        lax.fori_loop(0, OCC // 8, body, 0)

    def remote(src, dst, s_sem, r_sem, device):
        return pltpu.make_async_remote_copy(
            src_ref=src, dst_ref=dst, send_sem=s_sem, recv_sem=r_sem, device_id=device, device_id_type=MESH
        )

    sent = []

    def launch(copy):
        copy.start()
        sent.append(copy)
        return copy

    def arrived(ref, sem):
        pltpu.make_async_copy(ref, ref, sem).wait()

    def pack_first(s):
        for parity in range(2):
            for chain in (LONG, SHORT):
                base = (along(chain, parity, hops(chain)) * 2 + parity) * CAP
                for e in range(CAP):
                    send1[s, parity, chain, e] = scaled[s, 0, listed_at[ENTRY, 0, base + e]].astype(BF16)

    def send_first(s):
        for parity in range(2):
            for chain in (LONG, SHORT):
                launch(remote(
                    send1.at[s, parity, chain], recv1.at[s, chain, core],
                    s_one_s.at[s, parity, chain], s_one_r.at[s, chain, core],
                    (along(chain, parity, 1) * 2 + parity, ch),
                ))

    load[0].wait()
    to_scalars[0].wait()
    scale(0, 0)
    to_smem[ENTRY].wait()
    pack_first(0)

    for h in range(2):
        totals_t = jnp.dot(rw[...].astype(BF16), same[h].astype(F32).astype(BF16), preferred_element_type=F32)
        tile_totals[0, pl.ds(h * 128, 128), :] = totals_t.T

    pl.semaphore_wait(barrier, NCH + 4)

    smalls = [
        remote(src, dst, s_small_s.at[i], s_small_r.at[i], sibling)
        for i, (src, dst) in enumerate(
            ((lists.at[SLOT], lists.at[SLOT1]), (counts.at[0], counts.at[1]), (tile_totals.at[0], tile_totals.at[1]))
        )
    ]
    swaps = [remote(part_of(vis, s), v1.at[s], s_sib_s.at[s], s_sib_r.at[s], sibling) for s in range(PARTS)]
    send_first(0)
    launch(smalls[0])
    launch(smalls[1])
    launch(swaps[0])
    for side, near in ((0, above), (1, below)):
        for c in range(2):
            launch(remote(
                lists.at[RANK], lists.at[RANKS + side * 2 + core], s_rank_s.at[side, c], s_rank_r.at[side, core],
                (near * 2 + c, ch),
            ))
    launch(smalls[2])
    for copy in swaps[1:]:
        launch(copy)

    def local(s, tile):
        return scaled[s, 0, listed_at[SLOT, tile // 128, tile % 128]] + scaled[s, 1, listed_at[SLOT1, tile // 128, tile % 128]]

    ring, totals = {}, {}

    def emit(s, chain, h):
        owner_tiles = (along(chain, core, hops(chain) - h + 1) * 2 + core) * TPO
        if h > 2:
            ring[s, chain, h - 1].wait_recv()
        else:
            for c in range(2):
                arrived(recv1.at[s, chain, c], s_one_r.at[s, chain, c])
                got[c, 0:CAP] = recv1[s, chain, c].astype(F32)
        side = core if chain == LONG else 1 - core

        def body(g, carry):
            for j in range(8):
                i = g * 8 + j
                tile = owner_tiles + i
                acc = local(s, tile)
                if h > 2:
                    acc = acc + recv[s, chain, h - 3, i].astype(F32)
                else:
                    for c in range(2):
                        at = listed_at[RANKS + side * 2 + c, tile // 128, tile % 128]
                        acc = acc + got[c, at]
                send[s, chain, h - 2, i] = acc.astype(BF16)
            return carry

        lax.fori_loop(0, TPO // 8, body, 0)
        ring[s, chain, h] = launch(remote(
            send.at[s, chain, h - 2], recv.at[s, chain, h - 2],
            s_ring_s.at[s, chain, h - 2], s_ring_r.at[s, chain, h - 2], (along(chain, core, 1) * 2 + core, ch),
        ))

    def local_totals(owner_y):
        rows = pl.ds(pl.multiple_of((owner_y * 2 + core) * TPO, TPO), TPO)
        return tile_totals[0, rows, :] + tile_totals[1, rows, :]

    def emit_total(chain, h):
        acc = local_totals(along(chain, core, hops(chain) - h + 1))
        if h > 1:
            totals[chain, h - 1].wait_recv()
            acc = acc + trecv[chain, h - 2].astype(F32)
        tsend[chain, h - 1] = acc.astype(BF16)
        totals[chain, h] = launch(remote(
            tsend.at[chain, h - 1], trecv.at[chain, h - 1], s_tot_s.at[chain, h - 1], s_tot_r.at[chain, h - 1],
            (along(chain, core, 1) * 2 + core, ch),
        ))

    def total_inverse():
        acc = local_totals(y)
        for chain in (LONG, SHORT):
            totals[chain, hops(chain)].wait_recv()
            acc = acc + trecv[chain, hops(chain) - 1].astype(F32)
        square[0:TPO, :] = 1.0 / jnp.maximum(acc, 1.0)
        rinv[...] = square[...].T

    def settle(s):
        for chain in (LONG, SHORT):
            ring[s, chain, hops(chain)].wait_recv()
        factor = rinv[pl.ds(s * ROWS, ROWS), :]
        for i in range(TPO):
            acc = local(s, (y * 2 + core) * TPO + i)
            for chain in (LONG, SHORT):
                acc = acc + recv[s, chain, hops(chain) - 2, i].astype(F32)
            norm[i, s % 2] = acc * jnp.broadcast_to(factor[:, i : i + 1], (ROWS, 128))

    def exchange(g):
        for c in range(4):
            blocks = [norm[i, c // 2, (c % 2) * 8 : (c % 2) * 8 + 8, :] for i in range(TPO)]
            for group, block in enumerate(block_transpose(blocks, 8, 1)):
                mixed[group, c] = block
        for d in FAR_FIRST:
            group = (ch + d) % 16
            parts = block_transpose([mixed[group, c] for c in range(4)], 2, 0)
            for lh in range(2):
                outbox[g, lh * 16 + group] = jnp.concatenate([parts[lh], parts[2 + lh]], 0).astype(BF16)
            for to in (group, 16 + group) if d else ((ch + 16) % NCH,):
                remote(outbox.at[g, to], inbox.at[g, ch], s_a2a_s.at[g], s_a2a_r.at[g], (ob, to)).start()
        inbox[g, ch] = outbox[g, ch]

    def transform(g):
        arrived(inbox.at[g, pl.ds(0, NCH - 1)], s_a2a_r.at[g])
        if g == 0:
            load_tab.wait()
        cells = inbox[g].astype(F32).reshape(NCH, 2, 8, 128)
        for p in range(2):
            left = cells[:, p].reshape(NCH * 8, 128).T.astype(BF16)
            for b in range(2):
                right = jnp.concatenate([tabv[g, 3 * b + j] for j in range(3)], 1)
                block = jnp.dot(left, right, preferred_element_type=F32).reshape(TPO, 8, NCHAN)
                out[:, p, b] = block if g == 0 else out[:, p, b] + block

    def first(s):
        if s:
            load[s].wait()
            scale(s, 0)
            pack_first(s)
            send_first(s)

    def second(s):
        if s == 0:
            smalls[0].wait_recv()
            to_smem[SLOT1].start()
            smalls[1].wait_recv()
            to_scalars[1].start()
            for side in range(2):
                for c in range(2):
                    arrived(lists.at[RANKS + side * 2 + c], s_rank_r.at[side, c])
                    to_smem[RANKS + side * 2 + c].start()
            for i in range(LISTS):
                if i != ENTRY:
                    to_smem[i].wait()
            to_scalars[1].wait()
        swaps[s].wait_recv()
        scale(s, 1)

    def hop(s, h):
        for chain in (LONG, SHORT):
            if h <= hops(chain):
                emit(s, chain, h)
        if s == 0:
            if h == 2:
                smalls[2].wait_recv()
                emit_total(LONG, 1)
                emit_total(SHORT, 1)
            for chain in (LONG, SHORT):
                if h <= hops(chain):
                    emit_total(chain, h)

    def last(s):
        if s == 0:
            total_inverse()
        settle(s)
        if s % 2:
            exchange(s // 2)

    steps = []
    for s in range(PARTS):
        steps.append((FIRST * s, 0, s, first, (s,)))
        steps.append((s + HOP - SECOND, 1, s, second, (s,)))
        for h in range(2, 5):
            steps.append((s + HOP * (h - 1), h, s, hop, (s, h)))
        steps.append((s + HOP * 3 + LAST, 5, s, last, (s,)))
    for *_, step, which in sorted(steps, key=lambda step: step[:3]):
        step(*which)
    for g in range(GROUPS - 1):
        transform(g)
    for copy in sent:
        copy.wait_send()
    for g in range(GROUPS):
        arrived(outbox.at[g, pl.ds(0, NCH - 1)], s_a2a_s.at[g])
    transform(GROUPS - 1)


def shards(visibilities, weights, coverage, owner_map):
    vis = visibilities.reshape(OCC, LOCAL, 2, 2, 2, 128).transpose(0, 1, 2, 4, 3, 5).reshape(OCC, LOCAL * 8, 128)
    weights = weights[0].transpose(1, 2, 0).reshape(2 * LOCAL, OCC)
    small = jnp.pad(jnp.concatenate([weights, coverage], 0), ((0, 0), (0, 128 - OCC)))
    small = jnp.concatenate([small, owner_map.reshape(2, 128)], 0)
    table = jnp.asarray(delay_table())

    vmem, hbm = (pl.BlockSpec(memory_space=m) for m in (pltpu.VMEM, pltpu.HBM))
    dma = pltpu.SemaphoreType.DMA
    return pl.pallas_call(
        kernel,
        out_shape=jax.ShapeDtypeStruct((TPO, 2, 2, 8, NCHAN), F32),
        in_specs=[hbm, vmem, hbm],
        out_specs=vmem,
        scratch_shapes=[
            pltpu.VMEM((PARTS, OCC, ROWS, 128), BF16),
            pltpu.VMEM((PARTS, OCC, ROWS, 128), BF16),
            pltpu.VMEM((128, 128), F32),
            pltpu.VMEM((2, LOCAL, 2, 128), F32),
            pltpu.SMEM((2, LOCAL, 2, 128), F32),
            pltpu.VMEM((LISTS + 1, 2, 128), I32),
            pltpu.SMEM((LISTS, 2, 128), I32),
            pltpu.VMEM((2, 2 * 128, 128), F32),
            pltpu.VMEM((PARTS, 2, OCC + 1, ROWS, 128), F32),
            pltpu.VMEM((128, 128), F32),
            pltpu.VMEM((128, 128), F32),
            pltpu.VMEM((PARTS, 2, 2, CAP, ROWS, 128), BF16),
            pltpu.VMEM((PARTS, 2, 2, CAP, ROWS, 128), BF16),
            pltpu.VMEM((2, CAP + 1, ROWS, 128), F32),
            pltpu.VMEM((PARTS, 2, 3, TPO, ROWS, 128), BF16),
            pltpu.VMEM((PARTS, 2, 3, TPO, ROWS, 128), BF16),
            pltpu.VMEM((2, 4, TPO, 128), BF16),
            pltpu.VMEM((2, 4, TPO, 128), BF16),
            pltpu.VMEM((TPO, 2, ROWS, 128), F32),
            pltpu.VMEM((16, CPG, 8, 128), F32),
            pltpu.VMEM((GROUPS, NCH, 16, 128), BF16),
            pltpu.VMEM((GROUPS, NCH, 16, 128), BF16),
            pltpu.VMEM(table.shape, BF16),
            dma((PARTS,)),
            dma,
            dma((2,)),
            dma((LISTS,)),
            dma((PARTS,)),
            dma((PARTS,)),
            dma((3,)),
            dma((3,)),
            dma((2, 2)),
            dma((2, 2)),
            dma((PARTS, 2, 2)),
            dma((PARTS, 2, 2)),
            dma((PARTS, 2, 3)),
            dma((PARTS, 2, 3)),
            dma((2, 4)),
            dma((2, 4)),
            dma((GROUPS,)),
            dma((GROUPS,)),
        ],
        compiler_params=pltpu.CompilerParams(
            collective_id=0, has_side_effects=True, vmem_limit_bytes=53 * 1024 * 1024
        ),
    )(vis, small, table)


def solution(mesh):
    return jax.shard_map(
        shards,
        mesh=mesh,
        in_specs=(
            P("obs", None, "chan", None, None, None),
            P("obs", None, "chan", None),
            P("obs", None),
            P(),
        ),
        out_specs=P("obs", None, None, "chan", None),
        check_vma=False,
    )
```
